512 devices in a mesh: dp: 32 (over y, z_lo, core), tensor: 16 (over z_hi, x).
Axes of the slice: x: 4, y: 8, z: 8 (z_hi: 4, z_lo: 2; z = z_hi * 2 + z_lo), core: 2. Of those that a mesh axis runs over, the one named last changes fastest.
Arguments:
- tokens: bfloat16 [4096, 14336], P('dp', 'tensor'), may hold values from -22 to 22
- frozen_matrix: bfloat16 [14336, 4096], P('tensor', 'dp')
- adapter_down_factor: bfloat16 [14336, 64], P('tensor'), may hold values from -0.046875 to 0.046875
- adapter_up_factor: bfloat16 [64, 4096], P(None, 'tensor'), may hold values from -3 to 3
- magnitude: bfloat16 [4096], P('tensor'), may hold values from 0.5 to 2
- cotangent: bfloat16 [4096, 4096], P('dp'), may hold values from -6 to 6
Outputs:
- output: bfloat16 [4096, 4096], P('dp', 'tensor')
- input_gradient: bfloat16 [4096, 14336], P('dp', 'tensor')
- grad_down: float32 [14336, 64], P('tensor')
- grad_up: float32 [64, 4096], P(None, 'tensor')
- grad_magnitude: float32 [4096], P('tensor')
The draws below stay inside these ranges and needn't reach their ends.
All inputs are finite; a program needn't handle non-finite values.
Results may differ from the reference program's by a relative error of at most 0.0056.
Values may be sent and summed in bfloat16 or wider, within the bound.
No kernel may reach another device: no remote copies, remote signals or barrier semaphores. Data moves between devices by JAX's collectives and lax.ppermute only.
A program may use at most 64 MiB of HBM per device.

```python
import math
import jax
import jax.numpy as jnp
from jax import lax

OUTPUT_FEATURES = 4096
INPUT_FEATURES = 14336
ADAPTER_RANK = 64
TOKENS = 4096


def draw_tokens(key, part):
    key = jax.random.fold_in(key, 11)
    first, second = jax.random.split(key)
    values = jnp.clip(jax.random.normal(first, (TOKENS, INPUT_FEATURES), jnp.float32), -4.0, 4.0)
    trend = 3.0
    spread = jax.random.uniform(second, (TOKENS, 1), jnp.float32)
    position = jnp.arange(TOKENS, dtype=jnp.float32)[:, None] / max(TOKENS - 1, 1)
    row_scale = jnp.power(10.0, spread - 0.5) * jnp.power(trend, position - 0.5)
    return (values * row_scale).astype(jnp.bfloat16)


def draw_frozen_matrix(key, part):
    key = jax.random.fold_in(key, 23)
    first, second, third = jax.random.split(key, 3)
    values = jnp.clip(jax.random.normal(first, (INPUT_FEATURES, OUTPUT_FEATURES), jnp.float32), -4.0, 4.0)
    trend = 3.0
    row_spread = jax.random.uniform(second, (INPUT_FEATURES, 1), jnp.float32)
    column_spread = jax.random.uniform(third, (1, OUTPUT_FEATURES), jnp.float32)
    position = jnp.arange(INPUT_FEATURES, dtype=jnp.float32)[:, None] / max(INPUT_FEATURES - 1, 1)
    row_scale = jnp.power(10.0, row_spread - 0.5) * jnp.power(trend, position - 0.5)
    column_scale = jnp.power(10.0, column_spread - 0.5)
    return (values * row_scale * column_scale / jnp.sqrt(jnp.float32(INPUT_FEATURES))).astype(jnp.bfloat16)


def shard_levels(own_key, extent, cuts, smallest, largest):
    def one(dim, blocks):
        steps = jax.random.uniform(jax.random.fold_in(jax.random.fold_in(own_key, 6), dim), (blocks,), jnp.float32, smallest / len(cuts), largest / len(cuts))
        return jnp.repeat(jnp.exp(steps), extent[dim] // blocks).reshape((-1,) + (1,) * (len(extent) - dim - 1))

    factor_of = one(*cuts[0])
    for cut in cuts[1:]:
        factor_of = factor_of * one(*cut)
    return factor_of


def centred(key, extent, width, bound, cuts=(), kind=jnp.bfloat16):
    array = jax.random.normal(key, extent, jnp.float32) * width
    if len(cuts) > 0:
        array = shard_levels(key, extent, cuts, -0.22, 0.18) * array
    return jnp.clip(array, min=-bound, max=bound).astype(kind)


def setup_inputs(seed: int = 0) -> dict:
    keys = jax.random.split(jax.random.key(seed), 7)
    return {
        "tokens": draw_tokens(jax.random.fold_in(keys[6], 71), 0),
        "frozen_matrix": draw_frozen_matrix(jax.random.fold_in(keys[6], 71), 0),
        "adapter_down_factor": centred(keys[2], (INPUT_FEATURES, ADAPTER_RANK), INPUT_FEATURES ** -0.5, 0.046875, ((0, 16),)),
        "adapter_up_factor": centred(keys[3], (ADAPTER_RANK, OUTPUT_FEATURES), 4 ** -0.5, 3.0, ((1, 16),)),
        "magnitude": jnp.clip(jnp.exp(math.log(2.0) - 1.3862944 * jax.random.uniform(keys[4], (OUTPUT_FEATURES,), jnp.float32) ** shard_levels(keys[4], (OUTPUT_FEATURES,), ((0, 16),), -0.2, 0.2)), 0.5, 2.0).astype(jnp.bfloat16),
        "cotangent": centred(keys[5], (TOKENS, OUTPUT_FEATURES), 1.0, 6.0, ((0, 32),)),
    }


epsilon = 1e-06

def reference(tokens, frozen_matrix, adapter_down_factor, adapter_up_factor, magnitude, cotangent):
    rank_activation = jnp.dot(tokens, adapter_down_factor, preferred_element_type=jnp.float32).astype(jnp.bfloat16)
    combined_output = frozen_matrix.astype(jnp.float32) + jnp.dot(adapter_down_factor, adapter_up_factor, preferred_element_type=jnp.float32)
    squares = lax.optimization_barrier(jnp.sum(combined_output * combined_output, axis=0))
    norm = jnp.sqrt(squares + epsilon)
    scale = magnitude.astype(jnp.float32) / norm
    frozen_output = jnp.dot(tokens, frozen_matrix, preferred_element_type=jnp.float32)
    merged_weight = frozen_output + jnp.dot(rank_activation, adapter_up_factor, preferred_element_type=jnp.float32)
    output = (merged_weight * scale).astype(jnp.bfloat16)
    rescaled_gradient = (cotangent.astype(jnp.float32) * scale).astype(jnp.bfloat16)
    rank_gradient = jnp.dot(rescaled_gradient, adapter_up_factor.T, preferred_element_type=jnp.float32).astype(jnp.bfloat16)
    input_gradient = jnp.dot(rescaled_gradient, frozen_matrix.T, preferred_element_type=jnp.float32)
    input_gradient = (input_gradient + jnp.dot(rank_gradient, adapter_down_factor.T, preferred_element_type=jnp.float32)).astype(jnp.bfloat16)
    factor = 1.0 / jnp.sqrt(jnp.float32(TOKENS))
    grad_down = jnp.dot(tokens.T, rank_gradient, preferred_element_type=jnp.float32) * factor
    grad_up = jnp.dot(rank_activation.T, rescaled_gradient, preferred_element_type=jnp.float32) * factor
    grad_magnitude = lax.optimization_barrier(jnp.sum(cotangent.astype(jnp.float32) * merged_weight / norm, axis=0)) * factor
    return (output, input_gradient, grad_down, grad_up, grad_magnitude)
```

```python
import functools
import math

import jax
import jax.numpy as jnp
from jax import lax
from jax.experimental import pallas as pl
from jax.experimental.pallas import tpu as pltpu
from jax.sharding import PartitionSpec as P

epsilon = 1e-06
F32 = jnp.float32
BF16 = jnp.bfloat16


def spread(block, axis):
    n = lax.axis_size(axis)
    return lax.all_to_all(jnp.broadcast_to(block[None], (n,) + block.shape), axis, 0, 0)


def forward_kernel(x_ref, w_ref, y_ref):
    for h in range(2):
        y_ref[0, :, h * 128 : (h + 1) * 128] = jnp.dot(
            x_ref[...], w_ref[h], preferred_element_type=F32
        ).astype(BF16)


def forward(x, gathered):
    t, f = x.shape
    n = gathered.shape[0]
    return pl.pallas_call(
        forward_kernel,
        grid=(n // 2,),
        in_specs=[
            pl.BlockSpec((t, f), lambda i: (0, 0)),
            pl.BlockSpec((2, f, 128), lambda i: (i, 0, 0)),
        ],
        out_specs=pl.BlockSpec((1, t, 256), lambda i: (i, 0, 0)),
        out_shape=jax.ShapeDtypeStruct((n // 2, t, 256), BF16),
        cost_estimate=pl.CostEstimate(
            flops=2 * t * f * n * 128, bytes_accessed=2 * f * n * 128, transcendentals=0
        ),
        name="forward",
    )(x, gathered)


def backward_kernel(g_ref, w_ref, r_ref, a_ref, o_ref, acc):
    i = pl.program_id(0)
    dims = (((1,), (1,)), ((), ()))

    @pl.when(i == 0)
    def _():
        acc[...] = lax.dot_general(r_ref[...], a_ref[...], dims, preferred_element_type=F32)

    wide = jnp.concatenate([w_ref[0], w_ref[1]], axis=1)
    acc[...] += lax.dot_general(g_ref[...], wide, dims, preferred_element_type=F32)

    @pl.when(i == pl.num_programs(0) - 1)
    def _():
        o_ref[...] = acc[...].astype(BF16)


def backward(g, gathered, r, a):
    t = g.shape[0]
    n, f, _ = gathered.shape
    return pl.pallas_call(
        backward_kernel,
        grid=(n // 2,),
        in_specs=[
            pl.BlockSpec((t, 256), lambda i: (0, i)),
            pl.BlockSpec((2, f, 128), lambda i: (i, 0, 0)),
            pl.BlockSpec(r.shape, lambda i: (0, 0)),
            pl.BlockSpec(a.shape, lambda i: (0, 0)),
        ],
        out_specs=pl.BlockSpec((t, f), lambda i: (0, 0)),
        out_shape=jax.ShapeDtypeStruct((t, f), BF16),
        scratch_shapes=[pltpu.VMEM((t, f), F32)],
        cost_estimate=pl.CostEstimate(
            flops=2 * t * f * n * 128, bytes_accessed=2 * f * n * 128, transcendentals=0
        ),
        name="backward",
    )(g, gathered, r, a)


def on_device(tokens, frozen_matrix, adapter_down_factor, adapter_up_factor, magnitude, cotangent):
    t, f = tokens.shape
    n_dp, n_tp = lax.axis_size("dp"), lax.axis_size("tensor")
    p, q = lax.axis_index("dp"), lax.axis_index("tensor")
    rank, own = adapter_up_factor.shape
    half = f // 2

    gathered = lax.all_gather(frozen_matrix, "dp", axis=0)

    rank_partial = lax.dot_general(
        adapter_down_factor, tokens, (((0,), (1,)), ((), ())), preferred_element_type=F32
    ).astype(BF16)
    first = jnp.concatenate(
        [
            adapter_up_factor[:, :128],
            adapter_up_factor[:, 128:],
            rank_partial,
            magnitude.reshape(2, 128),
            jnp.zeros((14, 128), BF16),
        ],
        axis=0,
    )
    first = spread(first, "tensor")
    up_blocks = first[:, : 2 * rank].reshape(2 * n_tp, rank, 128)
    full_up = jnp.moveaxis(up_blocks, 0, 1).reshape(rank, -1)
    full_magnitude = first[:, 3 * rank : 3 * rank + 2].reshape(-1)
    rank_activation = jnp.sum(first[:, 2 * rank : 3 * rank].astype(F32), axis=0).astype(BF16)

    own_up = lax.dynamic_index_in_dim(up_blocks, p, 0, keepdims=False)
    combined = frozen_matrix.astype(F32) + jnp.dot(
        adapter_down_factor, own_up, preferred_element_type=F32
    )
    squares = jnp.sum(combined * combined, axis=0, keepdims=True)
    squares = jnp.sum(spread(squares, "tensor"), axis=0)
    squares = spread(squares, "dp").reshape(-1)
    norm = jnp.sqrt(squares + epsilon)
    scale = full_magnitude.astype(F32) / norm

    scaled = (cotangent.astype(F32) * scale).astype(BF16)
    rank_back = lax.dot_general(
        scaled, full_up, (((1,), (1,)), ((), ())), preferred_element_type=F32
    ).astype(BF16)
    down = lax.dot_general(
        tokens, rank_back, (((0,), (0,)), ((), ())), preferred_element_type=F32
    )
    start = q * own
    own_scaled = lax.dynamic_slice_in_dim(scaled, start, own, 1)
    up = jnp.dot(rank_activation, own_scaled, preferred_element_type=F32)
    shares = jnp.concatenate(
        [jnp.concatenate([down[:half], down[half:]], axis=1), up[:, :128], up[:, 128:]], axis=0
    ).astype(BF16)
    rows = shares.shape[0] // n_dp
    shares = lax.all_to_all(shares.reshape(n_dp, rows, 128), "dp", 0, 0)
    shares = jnp.sum(shares.astype(F32), axis=0)

    parts = lax.all_to_all(forward(tokens, gathered), "tensor", 0, 0)
    input_gradient = backward(scaled, gathered, rank_back, adapter_down_factor)
    merged = jnp.sum(parts.astype(F32), axis=0) + lax.dot_general(
        rank_activation, adapter_up_factor, (((0,), (0,)), ((), ())), preferred_element_type=F32
    )
    own_scale = lax.dynamic_slice_in_dim(scale, start, own, 0)
    own_norm = lax.dynamic_slice_in_dim(norm, start, own, 0)
    own_cotangent = lax.dynamic_slice_in_dim(cotangent, start, own, 1).astype(F32)
    output = (merged * own_scale).astype(BF16)
    mag_part = jnp.sum(own_cotangent * merged, axis=0) / own_norm

    high = mag_part.astype(BF16)
    low = (mag_part - high.astype(F32)).astype(BF16)
    last = jnp.concatenate(
        [shares.astype(BF16), high.reshape(2, 128), low.reshape(2, 128)], axis=0
    )
    last = spread(last, "dp").astype(F32)
    factor = 1.0 / math.sqrt(t * n_dp)
    sums = last[:, :rows].reshape(-1, 128) * factor
    grad_down = jnp.concatenate([sums[:half, :rank], sums[:half, rank:]], axis=0)
    grad_up = jnp.concatenate([sums[half : half + rank], sums[half + rank :]], axis=1)
    mags = jnp.sum(last[:, rows : rows + 2] + last[:, rows + 2 : rows + 4], axis=0)
    grad_magnitude = mags.reshape(-1) * factor
    return (output, input_gradient, grad_down, grad_up, grad_magnitude)


def solution(mesh):
    return jax.shard_map(
        on_device,
        mesh=mesh,
        in_specs=(
            P("dp", "tensor"),
            P("tensor", "dp"),
            P("tensor", None),
            P(None, "tensor"),
            P("tensor"),
            P("dp", None),
        ),
        out_specs=(
            P("dp", "tensor"),
            P("dp", "tensor"),
            P("tensor", None),
            P(None, "tensor"),
            P("tensor"),
        ),
        check_vma=False,
    )
```

```python
import math

import jax
import jax.numpy as jnp
from jax import lax
from jax.experimental import pallas as pl
from jax.experimental.pallas import tpu as pltpu
from jax.sharding import Mesh
from jax.sharding import PartitionSpec as P

epsilon = 1e-06
F32 = jnp.float32
BF16 = jnp.bfloat16
DP = ("y", "w", "c")
TP = ("z", "u", "v")


def spread(block, axis):
    n = lax.axis_size(axis)
    return lax.all_to_all(jnp.broadcast_to(block[None], (n,) + block.shape), axis, 0, 0)


def forward_kernel(x_ref, w_ref, y_ref):
    t = x_ref.shape[0] // 2
    for k in range(w_ref.shape[0] // 2):
        wide = jnp.concatenate([w_ref[2 * k], w_ref[2 * k + 1]], axis=1)
        y = jnp.dot(x_ref[...], wide, preferred_element_type=F32).astype(BF16)
        y_ref[2 * k] = y[:t]
        y_ref[2 * k + 1] = y[t:]


def forward(x, gathered, step=4):
    t, f = x.shape
    n = gathered.shape[0]
    return pl.pallas_call(
        forward_kernel,
        grid=(n // step,),
        in_specs=[
            pl.BlockSpec((t, f), lambda i: (0, 0)),
            pl.BlockSpec((step, f, 128), lambda i: (i, 0, 0)),
        ],
        out_specs=pl.BlockSpec((step, t // 2, 256), lambda i: (i, 0, 0)),
        out_shape=jax.ShapeDtypeStruct((n, t // 2, 256), BF16),
        cost_estimate=pl.CostEstimate(
            flops=2 * t * f * n * 128, bytes_accessed=2 * f * n * 128, transcendentals=0
        ),
        name="forward",
    )(x, gathered)


def backward_kernel(g_ref, h_ref, w_ref, r_ref, a_ref, own_ref, other_ref, acc):
    i = pl.program_id(0)
    dims = (((1,), (1,)), ((), ()))
    t = g_ref.shape[0]

    @pl.when(i == 0)
    def _():
        acc[:t] = lax.dot_general(r_ref[...], a_ref[...], dims, preferred_element_type=F32)
        acc[t:] = jnp.zeros_like(acc[t:])

    n = w_ref.shape[0]
    wide = jnp.concatenate([w_ref[k] for k in range(n)], axis=1)
    g = jnp.concatenate([g_ref[...], h_ref[...]], axis=0)
    acc[...] += lax.dot_general(g, wide, dims, preferred_element_type=F32)

    @pl.when(i == pl.num_programs(0) - 1)
    def _():
        own_ref[...] = acc[:t]
        other_ref[...] = acc[t:].astype(BF16)


def backward(g, h, gathered, r, a, step=4):
    t = g.shape[0]
    n, f, _ = gathered.shape
    return pl.pallas_call(
        backward_kernel,
        grid=(n // step,),
        in_specs=[
            pl.BlockSpec((t, step * 128), lambda i: (0, i)),
            pl.BlockSpec((t, step * 128), lambda i: (0, i)),
            pl.BlockSpec((step, f, 128), lambda i: (i, 0, 0)),
            pl.BlockSpec(r.shape, lambda i: (0, 0)),
            pl.BlockSpec(a.shape, lambda i: (0, 0)),
        ],
        out_specs=[pl.BlockSpec((t, f), lambda i: (0, 0))] * 2,
        out_shape=[
            jax.ShapeDtypeStruct((t, f), F32),
            jax.ShapeDtypeStruct((t, f), BF16),
        ],
        scratch_shapes=[pltpu.VMEM((2 * t, f), F32)],
        cost_estimate=pl.CostEstimate(
            flops=4 * t * f * n * 128, bytes_accessed=2 * f * n * 128, transcendentals=0
        ),
        name="backward",
    )(g, h, gathered, r, a)


def swap(x, axis):
    return lax.ppermute(x, axis, [(0, 1), (1, 0)])


def cross(x):
    return lax.ppermute(x, ("w", "v"), [(0, 0), (1, 2), (2, 1), (3, 3)])


def every_other(x, which):
    n = x.shape[-1] // 256
    pick = lambda s: jnp.concatenate(
        [x[..., i * 256 : (i + 1) * 256] for i in range(s, n, 2)], axis=-1
    )
    return jnp.where(which == 0, pick(0), pick(1))


def in_order(which, own, other, axis):
    return jnp.where(
        which == 0,
        jnp.concatenate([own, other], axis=axis),
        jnp.concatenate([other, own], axis=axis),
    )


def on_device(tokens, frozen_matrix, adapter_down_factor, adapter_up_factor, magnitude, cotangent):
    t, f = tokens.shape
    n_dp, n_tp = lax.axis_size(DP), lax.axis_size(TP)
    y, w, c, z, u, v = (lax.axis_index(a) for a in DP + TP)
    rank, own = adapter_up_factor.shape
    half = f // 2

    gathered = lax.all_gather(frozen_matrix, ("y", "c"), axis=0)
    other_tokens = swap(tokens, "w")
    own_cotangent = every_other(cotangent, w)
    other_cotangent = swap(every_other(cotangent, 1 - w), "w")

    rank_partial = lax.dot_general(
        adapter_down_factor, tokens, (((0,), (1,)), ((), ())), preferred_element_type=F32
    ).astype(BF16)
    first = jnp.concatenate(
        [
            jnp.where(c == 0, adapter_up_factor[:, :128], adapter_up_factor[:, 128:]),
            rank_partial,
            magnitude.reshape(2, 128),
            jnp.zeros((6, 128), BF16),
        ],
        axis=0,
    )
    first = spread(first, TP)
    own_half = first[:, :rank]
    full_magnitude = first[:, 2 * rank : 2 * rank + 2].reshape(-1)
    rank_activation = jnp.sum(first[:, rank : 2 * rank].astype(F32), axis=0).astype(BF16)
    other_rank_activation = swap(rank_activation, "w")
    other_half = swap(own_half, "c")
    up_blocks = in_order(c, own_half[:, None], other_half[:, None], 1)
    full_up = jnp.moveaxis(up_blocks, 2, 0).reshape(rank, -1)

    own_up = lax.dynamic_index_in_dim(own_half, 2 * y + w, 0, keepdims=False)
    combined = frozen_matrix.astype(F32) + jnp.dot(
        adapter_down_factor, own_up, preferred_element_type=F32
    )
    squares = jnp.sum(combined * combined, axis=0, keepdims=True)
    squares = jnp.sum(spread(squares, TP), axis=0)
    squares = spread(squares, DP).reshape(-1)
    norm = jnp.sqrt(squares + epsilon)
    scale = full_magnitude.astype(F32) / norm

    scaled = (cotangent.astype(F32) * scale).astype(BF16)
    rank_back = lax.dot_general(
        scaled, full_up, (((1,), (1,)), ((), ())), preferred_element_type=F32
    ).astype(BF16)
    down = lax.dot_general(
        tokens, rank_back, (((0,), (0,)), ((), ())), preferred_element_type=F32
    )
    q = (2 * z + u) * 2 + v
    up = jnp.dot(
        rank_activation,
        lax.dynamic_slice_in_dim(scaled, q * own, own, 1),
        preferred_element_type=F32,
    )
    shares = jnp.concatenate(
        [jnp.concatenate([down[:half], down[half:]], axis=1), up[:, :128], up[:, 128:]], axis=0
    ).astype(BF16)
    rows = shares.shape[0] // n_dp
    shares = lax.all_to_all(shares.reshape(n_dp, rows, 128), DP, 0, 0)
    shares = jnp.sum(shares.astype(F32), axis=0).astype(BF16)
    factor = 1.0 / math.sqrt(t * n_dp)
    sums = spread(shares, DP).astype(F32).reshape(-1, 128) * factor
    grad_down = jnp.concatenate([sums[:half, :rank], sums[:half, rank:]], axis=0)
    grad_up = jnp.concatenate([sums[half : half + rank], sums[half + rank :]], axis=1)

    other_scaled = (other_cotangent.astype(F32) * every_other(scale, w)).astype(BF16)
    own_part, other_part = backward(
        every_other(scaled, w), other_scaled, gathered, rank_back, adapter_down_factor
    )
    input_gradient = (own_part + swap(other_part, "w").astype(F32)).astype(BF16)

    parts = lax.all_to_all(forward(in_order(w, tokens, other_tokens, 0), gathered), TP, 0, 0)
    block = 2 * z + u
    here = 2 * block + w
    at = lambda x: lax.dynamic_slice_in_dim(x, here * own, own, 0)
    here_up = lax.dynamic_index_in_dim(up_blocks, here, 0, keepdims=False)
    here_rank = jnp.where(v == w, rank_activation, other_rank_activation)
    adapter = [
        lax.dot_general(here_rank, here_up[h], (((0,), (0,)), ((), ())), preferred_element_type=F32)
        for h in range(2)
    ]
    merged = jnp.sum(parts.astype(F32), axis=0) + jnp.concatenate(adapter, axis=1)
    output = cross((merged * at(scale)).astype(BF16))
    here_cotangent = lax.dynamic_slice_in_dim(
        jnp.where(v == w, own_cotangent, other_cotangent), block * own, own, 1
    ).astype(F32)
    mag_part = jnp.sum(here_cotangent * merged, axis=0) / at(norm)
    mags = spread(mag_part.reshape(2, 128), DP + ("v",))
    mags = mags.reshape(lax.axis_size("y"), 2, 4, 2, 128)
    mags = jnp.where(v == 0, mags[:, 0], mags[:, 1])
    grad_magnitude = jnp.sum(mags, axis=(0, 1)).reshape(-1) * factor
    return (output, input_gradient, grad_down, grad_up, grad_magnitude)


def solution(mesh):
    fine = Mesh(mesh.devices.reshape(8, 2, 2, 4, 2, 2), DP + TP)
    return jax.shard_map(
        on_device,
        mesh=fine,
        in_specs=(P(DP, TP), P(TP, DP), P(TP, None), P(None, TP), P(TP), P(DP, None)),
        out_specs=(P(DP, TP), P(DP, TP), P(TP, None), P(None, TP), P(TP)),
        check_vma=False,
    )
```

```python
import math

import jax
import jax.numpy as jnp
from jax import lax
from jax.experimental import pallas as pl
from jax.experimental.pallas import tpu as pltpu
from jax.sharding import Mesh
from jax.sharding import PartitionSpec as P

epsilon = 1e-06
F32 = jnp.float32
BF16 = jnp.bfloat16
DP = ("y", "w", "c")
TP = ("z", "u", "v")


def spread(block, axis):
    n = lax.axis_size(axis)
    return lax.all_to_all(jnp.broadcast_to(block[None], (n,) + block.shape), axis, 0, 0)


def forward_kernel(i_ref, x_ref, o_ref, a_ref, b_ref, c_ref, w_ref, *rest):
    u, v, w, c = (i_ref[k] for k in (0, 1, 3, 4))
    out, (x, r) = rest[:4], rest[4:]
    t = x_ref.shape[0]

    @pl.when(pl.program_id(0) == 0)
    def _():
        same = v == w
        x[:t] = jnp.where(same, x_ref[...], o_ref[...])
        x[t:] = jnp.where(same, o_ref[...], x_ref[...])
        r[...] = lax.dot_general(
            x[...], a_ref[...], (((1,), (1,)), ((), ())), preferred_element_type=F32
        ).astype(BF16)

    for k in range(2):
        at = (u + k) % 2
        b, d = b_ref[2 * at + w], c_ref[2 * at + w]
        up = jnp.concatenate([jnp.where(c == 0, b, d), jnp.where(c == 0, d, b)], axis=1)
        wide = jnp.concatenate([w_ref[2 * at], w_ref[2 * at + 1]], axis=1)
        y = jnp.dot(x[...], wide, preferred_element_type=F32)
        y = (y + jnp.dot(r[...], up, preferred_element_type=F32)).astype(BF16)
        out[2 * k][0] = y[:t]
        out[2 * k + 1][0] = y[t:]


def forward(place, x, other_x, down_t, up, other_up, gathered):
    t, f = x.shape
    n, rank = gathered.shape[0], down_t.shape[0]
    n_z = n // 4
    whole = lambda i, s: (0, 0)
    part = lambda i, s: (i, 0, 0)
    return pl.pallas_call(
        forward_kernel,
        grid_spec=pltpu.PrefetchScalarGridSpec(
            num_scalar_prefetch=1,
            grid=(n_z,),
            in_specs=[
                pl.BlockSpec((t, f), whole),
                pl.BlockSpec((t, f), whole),
                pl.BlockSpec((rank, f), whole),
                pl.BlockSpec((4, rank, 128), part),
                pl.BlockSpec((4, rank, 128), part),
                pl.BlockSpec((4, f, 128), part),
            ],
            out_specs=[pl.BlockSpec((1, t, 256), lambda i, s: ((i + n_z - s[2]) % n_z, 0, 0))] * 4,
            scratch_shapes=[pltpu.VMEM((2 * t, f), BF16), pltpu.VMEM((2 * t, rank), BF16)],
        ),
        out_shape=[jax.ShapeDtypeStruct((n_z, t, 256), BF16)] * 4,
        cost_estimate=pl.CostEstimate(
            flops=4 * t * f * n * 128, bytes_accessed=2 * f * n * 128, transcendentals=0
        ),
        name="forward",
    )(place, x, other_x, down_t, up, other_up, gathered)


def backward_kernel(i_ref, g_ref, h_ref, s_ref, w_ref, r_ref, a_ref, own_ref, other_ref, acc):
    i = pl.program_id(0)
    t = g_ref.shape[0]

    @pl.when(i == 0)
    def _():
        acc[:t] = jnp.dot(r_ref[...], a_ref[...], preferred_element_type=F32)
        acc[t:] = jnp.zeros_like(acc[t:])

    wide = jnp.concatenate([w_ref[0], w_ref[1]], axis=1)
    g = jnp.concatenate([g_ref[...], h_ref[...]], axis=0)
    g = (g.astype(F32) * s_ref[...]).astype(BF16)
    acc[...] += lax.dot_general(
        g, wide, (((1,), (1,)), ((), ())), preferred_element_type=F32
    )

    @pl.when(i == pl.num_programs(0) - 1)
    def _():
        own_ref[...] = acc[:t]
        other_ref[...] = acc[t:].astype(BF16)


def backward(place, cotangent, other_cotangent, scale, gathered, r, down_t):
    t = cotangent.shape[0]
    n, f, _ = gathered.shape
    whole = lambda i, s: (0, 0)
    mine = lambda i, s: (0, 2 * i + s[3])
    return pl.pallas_call(
        backward_kernel,
        grid_spec=pltpu.PrefetchScalarGridSpec(
            num_scalar_prefetch=1,
            grid=(n // 2,),
            in_specs=[
                pl.BlockSpec((t, 256), mine),
                pl.BlockSpec((t, 256), lambda i, s: (0, i)),
                pl.BlockSpec((1, 256), mine),
                pl.BlockSpec((2, f, 128), lambda i, s: (i, 0, 0)),
                pl.BlockSpec(r.shape, whole),
                pl.BlockSpec(down_t.shape, whole),
            ],
            out_specs=[pl.BlockSpec((t, f), whole)] * 2,
            scratch_shapes=[pltpu.VMEM((2 * t, f), F32)],
        ),
        out_shape=[
            jax.ShapeDtypeStruct((t, f), F32),
            jax.ShapeDtypeStruct((t, f), BF16),
        ],
        cost_estimate=pl.CostEstimate(
            flops=4 * t * f * n * 128, bytes_accessed=2 * f * n * 128, transcendentals=0
        ),
        name="backward",
    )(place, cotangent, other_cotangent, scale, gathered, r, down_t)


def swap(x, axis):
    return lax.ppermute(x, axis, [(0, 1), (1, 0)])


def cross(x):
    return lax.ppermute(x, ("w", "v"), [(0, 0), (1, 2), (2, 1), (3, 3)])


def every_other(x, which):
    n = x.shape[-1] // 256
    pick = lambda s: jnp.concatenate(
        [x[..., i * 256 : (i + 1) * 256] for i in range(s, n, 2)], axis=-1
    )
    return jnp.where(which == 0, pick(0), pick(1))


def in_order(which, own, other, axis):
    return jnp.where(
        which == 0,
        jnp.concatenate([own, other], axis=axis),
        jnp.concatenate([other, own], axis=axis),
    )


def second_kernel(i_ref, w_ref, a_ref, b_ref, x_ref, o_ref):
    rank = a_ref.shape[0]
    whole = w_ref[...].astype(F32) + lax.dot_general(
        a_ref[...], b_ref[0, :rank], (((0,), (0,)), ((), ())), preferred_element_type=F32
    )
    left = jnp.sum(whole * whole, axis=0, keepdims=True)
    pieces = []
    for _ in range(3):
        pieces.append(left.astype(BF16))
        left = left - pieces[-1].astype(F32)
    pieces.append(jnp.zeros((5, 128), BF16))
    r = lax.dot_general(
        a_ref[...], x_ref[...], (((1,), (1,)), ((), ())), preferred_element_type=F32
    )
    o_ref[...] = jnp.concatenate([r.astype(BF16)] + pieces, axis=0)


def second_block(index, w, down_t, first, tokens):
    rows, (rank, f) = first.shape[1], down_t.shape
    whole = lambda i, s: (0, 0)
    return pl.pallas_call(
        second_kernel,
        grid_spec=pltpu.PrefetchScalarGridSpec(
            num_scalar_prefetch=1,
            grid=(1,),
            in_specs=[
                pl.BlockSpec(w.shape, whole),
                pl.BlockSpec(down_t.shape, whole),
                pl.BlockSpec((1, rows, 128), lambda i, s: (s[0], 0, 0)),
                pl.BlockSpec(tokens.shape, whole),
            ],
            out_specs=pl.BlockSpec((rank + 8, 128), whole),
        ),
        out_shape=jax.ShapeDtypeStruct((rank + 8, 128), BF16),
        name="second_block",
    )(index.reshape(1), w, down_t, first, tokens)


def on_device(tokens, frozen_matrix, adapter_down_factor, adapter_up_factor, magnitude, cotangent):
    t, f = tokens.shape
    n_dp, n_tp = lax.axis_size(DP), lax.axis_size(TP)
    y, w, c, z, u, v = (lax.axis_index(a) for a in DP + TP)
    rank, own = adapter_up_factor.shape
    down_t = adapter_down_factor.T
    place = jnp.stack([u, v, z, w, c])
    tie = lax.optimization_barrier

    gathered = lax.all_gather(frozen_matrix, ("y", "c"), axis=0)

    first = jnp.concatenate(
        [
            jnp.where(c == 0, adapter_up_factor[:, :128], adapter_up_factor[:, 128:]),
            magnitude.reshape(2, 128),
            jnp.zeros((6, 128), BF16),
        ],
        axis=0,
    )
    first = spread(first, TP)
    cotangent_out = every_other(cotangent, 1 - w)
    cotangent_out, tokens_out = tie((cotangent_out, tokens))
    other_tokens = swap(tokens_out, "w")

    second = second_block(2 * y + w, frozen_matrix, down_t, first, tokens)
    second, cotangent_out, first = tie((second, cotangent_out, first))
    second = spread(second, TP).astype(F32)
    rank_activation = jnp.sum(second[:, :rank], axis=0).astype(BF16)
    squares = jnp.sum(second[:, rank : rank + 3], axis=(0, 1)).reshape(1, 128)
    own_half = first[:, :rank]
    other_half = swap(own_half, "c")
    full_magnitude = first[:, rank : rank + 2].reshape(-1)
    up_blocks = in_order(c, own_half[:, None], other_half[:, None], 1)
    full_up = jnp.moveaxis(up_blocks, 2, 0).reshape(rank, -1)

    squares = spread(squares, DP)
    other_cotangent = swap(cotangent_out, "w")
    outgoing = forward(place, tokens, other_tokens, down_t, own_half, other_half, gathered)
    squares, outgoing = tie((squares, outgoing))
    received = [
        lax.ppermute(outgoing[k], ("u", "v"), [(i, i ^ k) for i in range(4)]) for k in (1, 2, 3)
    ]
    along_x = sum((r.astype(F32) for r in received), outgoing[0].astype(F32))
    n_z = lax.axis_size("z")
    along_z = [along_x[0]] + [
        lax.ppermute(
            along_x[k].astype(BF16), "z", [(i, (i + k) % n_z) for i in range(n_z)]
        ).astype(F32)
        for k in range(1, n_z)
    ]

    norm = jnp.sqrt(squares.reshape(-1) + epsilon)
    scale = full_magnitude.astype(F32) / norm
    scaled = (cotangent.astype(F32) * scale).astype(BF16)
    rank_back = lax.dot_general(
        scaled, full_up, (((1,), (1,)), ((), ())), preferred_element_type=F32
    ).astype(BF16)
    down = lax.dot_general(
        rank_back, tokens, (((0,), (0,)), ((), ())), preferred_element_type=F32
    )
    q = (2 * z + u) * 2 + v
    up = jnp.dot(
        rank_activation,
        lax.dynamic_slice_in_dim(scaled, q * own, own, 1),
        preferred_element_type=F32,
    )
    columns = [down[:, i : i + 128] for i in range(0, f, 128)]
    columns += [up[:, i : i + 128] for i in range(0, own, 128)]
    shares = jnp.concatenate(columns, axis=0).astype(BF16)
    shares = lax.all_to_all(shares.reshape(n_dp, -1, 128), DP, 0, 0)
    shares = jnp.sum(shares.astype(F32), axis=0).astype(BF16)

    block = 2 * z + u
    here = 2 * block + w
    at = lambda x: lax.dynamic_slice_in_dim(x, here * own, own, 0)
    merged = sum(along_z[1:], along_z[0])
    here_cotangent = jnp.where(
        v == w,
        lax.dynamic_slice_in_dim(cotangent, here * own, own, 1),
        lax.dynamic_slice_in_dim(other_cotangent, block * own, own, 1),
    ).astype(F32)
    mag_part = jnp.sum(here_cotangent * merged, axis=0) / at(norm)

    rows = shares.shape[0]
    high = lax.reduce_precision(mag_part, 8, 7)
    last = jnp.concatenate(
        [
            shares,
            high.astype(BF16).reshape(2, 128),
            (mag_part - high).astype(BF16).reshape(2, 128),
        ],
        axis=0,
    )
    last, merged, rank_back = tie((last, merged, rank_back))
    last = spread(last, DP + ("v",)).reshape(n_dp // 4, 2, 2, 2, rows + 4, 128)
    factor = 1.0 / math.sqrt(t * n_dp)
    sums = jnp.where(v == 0, last[:, :, :, 0, :rows], last[:, :, :, 1, :rows])
    sums = sums.astype(F32).reshape(-1, rank, 128) * factor
    grad_down = jnp.concatenate([sums[i] for i in range(f // 128)], axis=1).T
    grad_up = jnp.concatenate([sums[i] for i in range(f // 128, sums.shape[0])], axis=1)
    mags = jnp.where(v == 0, last[:, 0, :, :, rows:], last[:, 1, :, :, rows:]).astype(F32)
    mags = jnp.sum(mags, axis=(0, 1, 2))
    grad_magnitude = (mags[:2] + mags[2:]).reshape(-1) * factor

    output = cross((merged * at(scale)).astype(BF16))
    own_part, other_part = backward(
        place, cotangent, other_cotangent, scale.reshape(1, -1), gathered, rank_back, down_t
    )
    input_gradient = (own_part + swap(other_part, "w").astype(F32)).astype(BF16)
    return (output, input_gradient, grad_down, grad_up, grad_magnitude)


def solution(mesh):
    fine = Mesh(mesh.devices.reshape(8, 2, 2, 4, 2, 2), DP + TP)
    return jax.shard_map(
        on_device,
        mesh=fine,
        in_specs=(P(DP, TP), P(TP, DP), P(TP, None), P(None, TP), P(TP), P(DP, None)),
        out_specs=(P(DP, TP), P(DP, TP), P(TP, None), P(None, TP), P(TP)),
        check_vma=False,
    )
```

```python
import math

import jax
import jax.numpy as jnp
from jax import lax
from jax.experimental import pallas as pl
from jax.experimental.pallas import tpu as pltpu
from jax.sharding import Mesh
from jax.sharding import PartitionSpec as P

epsilon = 1e-06
F32 = jnp.float32
BF16 = jnp.bfloat16
DP = ("g", "h", "w", "c")
TP = ("z", "u", "v")


def spread(block, axis):
    n = lax.axis_size(axis)
    return lax.all_to_all(jnp.broadcast_to(block[None], (n,) + block.shape), axis, 0, 0)


def forward_kernel(i_ref, x_ref, o_ref, a_ref, b_ref, c_ref, w_ref, *rest):
    w, c = i_ref[0], i_ref[1]
    out, x, r = rest
    t = x_ref.shape[0]

    @pl.when(pl.program_id(0) == 0)
    def _():
        x[:t] = jnp.where(w == 0, x_ref[...], o_ref[...])
        x[t:] = jnp.where(w == 0, o_ref[...], x_ref[...])
        r[...] = lax.dot_general(
            x[...], a_ref[...], (((1,), (1,)), ((), ())), preferred_element_type=F32
        ).astype(BF16)

    for k in range(2):
        b, d = b_ref[2 * k + w], c_ref[2 * k + w]
        up = jnp.concatenate([jnp.where(c == 0, b, d), jnp.where(c == 0, d, b)], axis=1)
        wide = jnp.concatenate([w_ref[2 * k], w_ref[2 * k + 1]], axis=1)
        y = jnp.dot(x[...], wide, preferred_element_type=F32)
        y = (y + jnp.dot(r[...], up, preferred_element_type=F32)).astype(BF16)
        out[2 * k] = y[:t]
        out[2 * k + 1] = y[t:]


def forward(place, x, other_x, down_t, up, other_up, gathered):
    t, f = x.shape
    n, rank = gathered.shape[0], down_t.shape[0]
    whole = lambda i, s: (0, 0)
    part = lambda i, s: (i, 0, 0)
    return pl.pallas_call(
        forward_kernel,
        grid_spec=pltpu.PrefetchScalarGridSpec(
            num_scalar_prefetch=1,
            grid=(n // 4,),
            in_specs=[
                pl.BlockSpec((t, f), whole),
                pl.BlockSpec((t, f), whole),
                pl.BlockSpec((rank, f), whole),
                pl.BlockSpec((4, rank, 128), part),
                pl.BlockSpec((4, rank, 128), part),
                pl.BlockSpec((4, f, 128), part),
            ],
            out_specs=pl.BlockSpec((4, t, 256), part),
            scratch_shapes=[pltpu.VMEM((2 * t, f), BF16), pltpu.VMEM((2 * t, rank), BF16)],
        ),
        out_shape=jax.ShapeDtypeStruct((n, t, 256), BF16),
        cost_estimate=pl.CostEstimate(
            flops=4 * t * f * n * 128, bytes_accessed=2 * f * n * 128, transcendentals=0
        ),
        name="forward",
    )(place, x, other_x, down_t, up, other_up, gathered)


def backward_kernel(
    i_ref, g_ref, k_ref, h_ref, s_ref, q_ref, w_ref, r_ref, a_ref, own_ref, other_ref, acc
):
    i = pl.program_id(0)
    t = g_ref.shape[0]

    @pl.when(i == 0)
    def _():
        acc[:t] = jnp.dot(r_ref[...], a_ref[...], preferred_element_type=F32)
        acc[t:] = jnp.zeros_like(acc[t:])

    wide = jnp.concatenate([w_ref[k] for k in range(4)], axis=1)
    g = jnp.concatenate([g_ref[...], k_ref[...]], axis=1)
    g = jnp.concatenate([g, h_ref[...]], axis=0).astype(F32)
    g = (g * jnp.concatenate([s_ref[...], q_ref[...]], axis=1)).astype(BF16)
    acc[...] += lax.dot_general(
        g, wide, (((1,), (1,)), ((), ())), preferred_element_type=F32
    )

    @pl.when(i == pl.num_programs(0) - 1)
    def _():
        own_ref[...] = acc[:t]
        other_ref[...] = acc[t:].astype(BF16)


def backward(place, cotangent, other_cotangent, scale, gathered, r, down_t):
    t = cotangent.shape[0]
    n, f, _ = gathered.shape
    whole = lambda i, s: (0, 0)
    mine = lambda i, s: (0, 4 * i + s[0])
    next_mine = lambda i, s: (0, 4 * i + 2 + s[0])
    return pl.pallas_call(
        backward_kernel,
        grid_spec=pltpu.PrefetchScalarGridSpec(
            num_scalar_prefetch=1,
            grid=(n // 4,),
            in_specs=[
                pl.BlockSpec((t, 256), mine),
                pl.BlockSpec((t, 256), next_mine),
                pl.BlockSpec((t, 512), lambda i, s: (0, i)),
                pl.BlockSpec((1, 256), mine),
                pl.BlockSpec((1, 256), next_mine),
                pl.BlockSpec((4, f, 128), lambda i, s: (i, 0, 0)),
                pl.BlockSpec(r.shape, whole),
                pl.BlockSpec(down_t.shape, whole),
            ],
            out_specs=[pl.BlockSpec((t, f), whole)] * 2,
            scratch_shapes=[pltpu.VMEM((2 * t, f), F32)],
        ),
        out_shape=[
            jax.ShapeDtypeStruct((t, f), F32),
            jax.ShapeDtypeStruct((t, f), BF16),
        ],
        cost_estimate=pl.CostEstimate(flops=4 * t * f * n * 128, bytes_accessed=2 * f * n * 128, transcendentals=0),
        name="backward",
    )(place, cotangent, cotangent, other_cotangent, scale, scale, gathered, r, down_t)


def swap(x, axis):
    return lax.ppermute(x, axis, [(0, 1), (1, 0)])


def cross(x):
    return lax.ppermute(x, ("w", "v"), [(0, 0), (1, 2), (2, 1), (3, 3)])


def every_other(x, which):
    n = x.shape[-1] // 256
    pick = lambda s: jnp.concatenate(
        [x[..., i * 256 : (i + 1) * 256] for i in range(s, n, 2)], axis=-1
    )
    return jnp.where(which == 0, pick(0), pick(1))


def in_order(which, own, other, axis):
    return jnp.where(
        which == 0,
        jnp.concatenate([own, other], axis=axis),
        jnp.concatenate([other, own], axis=axis),
    )


def fold(x, axis, where):
    n = x.shape[0] // 2
    sent = swap(jnp.where(where == 0, x[n:], x[:n]), axis)
    return jnp.where(where == 0, x[:n], x[n:]) + sent


def scatter(x, axis, where):
    n = lax.axis_size(axis)
    x = x.reshape(n, x.shape[0] // n, x.shape[1])
    block = lambda k: lax.dynamic_index_in_dim(x, (where + k) % n, 0, keepdims=False)
    total = block(0)
    for k in range(1, n):
        total += lax.ppermute(block(k), axis, [(i, (i + k) % n) for i in range(n)])
    return total


def second_kernel(i_ref, w_ref, a_ref, b_ref, x_ref, m_ref, o_ref):
    rank = a_ref.shape[0]
    whole = w_ref[...].astype(F32) + lax.dot_general(
        a_ref[...], b_ref[0], (((0,), (0,)), ((), ())), preferred_element_type=F32
    )
    left = jnp.sum(whole * whole, axis=0, keepdims=True)
    pieces = []
    for _ in range(3):
        pieces.append(left.astype(BF16))
        left = left - pieces[-1].astype(F32)
    r = lax.dot_general(
        a_ref[...], x_ref[...], (((1,), (1,)), ((), ())), preferred_element_type=F32
    )
    tail = jnp.concatenate(pieces + [m_ref[...], jnp.zeros((11, 128), BF16)], axis=0)
    for i in range(o_ref.shape[0]):
        o_ref[i, :rank] = r.astype(BF16)
        o_ref[i, rank:] = tail


def second_blocks(index, w, down_t, up, tokens, magnitude):
    (n, rank, _), f = up.shape, down_t.shape[1]
    whole = lambda i, s: (0, 0)
    return pl.pallas_call(
        second_kernel,
        grid_spec=pltpu.PrefetchScalarGridSpec(
            num_scalar_prefetch=1,
            grid=(1,),
            in_specs=[
                pl.BlockSpec(w.shape, whole),
                pl.BlockSpec(down_t.shape, whole),
                pl.BlockSpec((1, rank, 128), lambda i, s: (s[0], 0, 0)),
                pl.BlockSpec(tokens.shape, whole),
                pl.BlockSpec((2, 128), whole),
            ],
            out_specs=pl.BlockSpec((n, rank + 16, 128), lambda i, s: (0, 0, 0)),
        ),
        out_shape=jax.ShapeDtypeStruct((n, rank + 16, 128), BF16),
        name="second_blocks",
    )(index.reshape(1), w, down_t, up, tokens, magnitude.reshape(2, 128))


def on_device(tokens, frozen_matrix, adapter_down_factor, adapter_up_factor, magnitude, cotangent):
    t, f = tokens.shape
    n_dp, n_tp = lax.axis_size(DP), lax.axis_size(TP)
    g, h, w, c, z, u, v = (lax.axis_index(a) for a in DP + TP)
    rank, own = adapter_up_factor.shape
    down_t = adapter_down_factor.T
    place = jnp.stack([w, c])
    tie = lax.optimization_barrier

    gathered = lax.all_gather(frozen_matrix, ("g", "h", "c"), axis=0)

    own_half = jnp.where(c == 0, adapter_up_factor[:, :128], adapter_up_factor[:, 128:])
    own_half = spread(own_half, TP)
    cotangent_out = every_other(cotangent, 1 - w)
    cotangent_out, tokens_out = tie((cotangent_out, tokens))
    other_tokens = swap(tokens_out, "w")

    index = (2 * g + h) * 2 + w
    second = second_blocks(index, frozen_matrix, down_t, own_half, tokens, magnitude)
    second, cotangent_out, own_half = tie((second, cotangent_out, own_half))
    second = lax.all_to_all(second, TP, 0, 0)
    squares = second[:, rank : rank + 3].astype(F32)
    squares = jnp.sum(squares, axis=(0, 1)).reshape(1, 128)
    other_half = swap(own_half, "c")
    up_blocks = in_order(c, own_half[:, None], other_half[:, None], 1)
    full_up = jnp.moveaxis(up_blocks, 2, 0).reshape(rank, -1)

    squares = spread(squares, DP)
    rank_activation = jnp.sum(second[:, :rank].astype(F32), axis=0).astype(BF16)
    full_magnitude = second[:, rank + 3 : rank + 5].reshape(-1)
    other_cotangent = swap(cotangent_out, "w")
    outgoing = forward(place, tokens, other_tokens, down_t, own_half, other_half, gathered)
    squares, outgoing, other_cotangent = tie((squares, outgoing, other_cotangent))

    parts = lax.all_to_all(outgoing, TP, 0, 0)

    norm = jnp.sqrt(squares.reshape(-1) + epsilon)
    scale = full_magnitude.astype(F32) / norm
    scaled = (cotangent.astype(F32) * scale).astype(BF16)
    rank_back = lax.dot_general(
        scaled, full_up, (((1,), (1,)), ((), ())), preferred_element_type=F32
    ).astype(BF16)
    down = lax.dot_general(
        rank_back, tokens, (((0,), (0,)), ((), ())), preferred_element_type=F32
    )
    q = (2 * z + u) * 2 + v
    up = jnp.dot(
        rank_activation,
        lax.dynamic_slice_in_dim(scaled, q * own, own, 1),
        preferred_element_type=F32,
    )
    shares = jnp.concatenate([down, up], axis=1)
    shares = fold(fold(shares, "c", c), "h", h)
    shares = scatter(shares, "g", g)

    shares, rank_back = tie((shares, rank_back))
    own_part, other_part = backward(
        place, cotangent, other_cotangent, scale.reshape(1, -1), gathered, rank_back, down_t
    )
    shares = fold(shares, "w", w)
    parts, other_part = tie((parts, other_part))

    block = 2 * z + u
    here = 2 * block + w
    at = lambda x: lax.dynamic_slice_in_dim(x, here * own, own, 0)
    merged = jnp.sum(parts.astype(F32), axis=0)
    here_cotangent = jnp.where(
        v == w,
        lax.dynamic_slice_in_dim(cotangent, here * own, own, 1),
        lax.dynamic_slice_in_dim(other_cotangent, block * own, own, 1),
    ).astype(F32)
    mag_part = jnp.sum(here_cotangent * merged, axis=0) / at(norm)

    high = lax.reduce_precision(mag_part, 8, 7)
    mag_part = jnp.stack([high, mag_part - high]).astype(BF16)
    last = jnp.concatenate([shares.astype(BF16), mag_part], axis=1)
    last, merged, other_part = tie((last, merged, other_part))
    last = spread(last, ("c", "h", "g", "w", "v")).reshape(n_dp // 2, 2, 2, 2, f + 2 * own)
    factor = 1.0 / math.sqrt(t * n_dp)
    sums = last[..., : f + own]
    sums = jnp.where(v == 0, sums[:, :, 0], sums[:, :, 1]).astype(F32)
    sums = sums.reshape(rank, f + own) * factor
    grad_down = sums[:, :f].T
    grad_up = sums[:, f:]
    mags = last[..., f + own :]
    mags = jnp.where(v == 0, mags[:, 0], mags[:, 1]).astype(F32)
    grad_magnitude = jnp.sum(mags, axis=(0, 1, 2)) * factor

    output = cross((merged * at(scale)).astype(BF16))
    input_gradient = (own_part + swap(other_part, "w").astype(F32)).astype(BF16)
    return (output, input_gradient, grad_down, grad_up, grad_magnitude)


def solution(mesh):
    fine = Mesh(mesh.devices.reshape(4, 2, 2, 2, 4, 2, 2), DP + TP)
    return jax.shard_map(
        on_device,
        mesh=fine,
        in_specs=(P(DP, TP), P(TP, DP), P(TP, None), P(None, TP), P(TP), P(DP, None)),
        out_specs=(P(DP, TP), P(DP, TP), P(TP, None), P(None, TP), P(TP)),
        check_vma=False,
    )
```

```python
import math

import jax
import jax.numpy as jnp
from jax import lax
from jax.experimental import pallas as pl
from jax.experimental.pallas import tpu as pltpu
from jax.sharding import Mesh
from jax.sharding import PartitionSpec as P

epsilon = 1e-06
F32 = jnp.float32
BF16 = jnp.bfloat16
DP = ("g", "h", "w", "c")
TP = ("z", "u", "v")


def spread(block, axis):
    n = lax.axis_size(axis)
    return lax.all_to_all(jnp.broadcast_to(block[None], (n,) + block.shape), axis, 0, 0)


def forward_kernel(i_ref, x_ref, o_ref, a_ref, b_ref, c_ref, w_ref, *rest):
    w, c = i_ref[0], i_ref[1]
    out, x, r = rest
    t = x_ref.shape[0]

    @pl.when(pl.program_id(0) == 0)
    def _():
        x[:t] = jnp.where(w == 0, x_ref[...], o_ref[...])
        x[t:] = jnp.where(w == 0, o_ref[...], x_ref[...])
        r[...] = lax.dot_general(
            x[...], a_ref[...], (((1,), (1,)), ((), ())), preferred_element_type=F32
        ).astype(BF16)

    for k in range(2):
        b, d = b_ref[2 * k + w], c_ref[2 * k + w]
        up = jnp.concatenate([jnp.where(c == 0, b, d), jnp.where(c == 0, d, b)], axis=1)
        wide = jnp.concatenate([w_ref[2 * k], w_ref[2 * k + 1]], axis=1)
        y = jnp.dot(x[...], wide, preferred_element_type=F32)
        y = (y + jnp.dot(r[...], up, preferred_element_type=F32)).astype(BF16)
        out[2 * k] = y[:t]
        out[2 * k + 1] = y[t:]


def forward(place, x, other_x, down_t, up, other_up, gathered):
    t, f = x.shape
    n, rank = gathered.shape[0], down_t.shape[0]
    whole = lambda i, s: (0, 0)
    part = lambda i, s: (i, 0, 0)
    return pl.pallas_call(
        forward_kernel,
        grid_spec=pltpu.PrefetchScalarGridSpec(
            num_scalar_prefetch=1,
            grid=(n // 4,),
            in_specs=[
                pl.BlockSpec((t, f), whole),
                pl.BlockSpec((t, f), whole),
                pl.BlockSpec((rank, f), whole),
                pl.BlockSpec((4, rank, 128), part),
                pl.BlockSpec((4, rank, 128), part),
                pl.BlockSpec((4, f, 128), part),
            ],
            out_specs=pl.BlockSpec((4, t, 256), part),
            scratch_shapes=[pltpu.VMEM((2 * t, f), BF16), pltpu.VMEM((2 * t, rank), BF16)],
        ),
        out_shape=jax.ShapeDtypeStruct((n, t, 256), BF16),
        cost_estimate=pl.CostEstimate(
            flops=4 * t * f * n * 128, bytes_accessed=2 * f * n * 128, transcendentals=0
        ),
        name="forward",
    )(place, x, other_x, down_t, up, other_up, gathered)


def backward_kernel(i_ref, g_ref, h_ref, s_ref, w_ref, r_ref, a_ref, own_ref, other_ref, acc):
    i, last = pl.program_id(0), pl.num_programs(0) - 1
    t, n = g_ref.shape[0], w_ref.shape[0]
    wide = jnp.concatenate([w_ref[k] for k in range(n)], axis=1)
    rows, scales = [], []
    for k in range(n // 2):
        mine = pl.ds(pl.multiple_of((n * i + 2 * k + i_ref[0]) * 256, 256), 256)
        rows.append(g_ref[:, mine])
        scales.append(s_ref[:, mine])
    g = jnp.concatenate([jnp.concatenate(rows, axis=1), h_ref[...]], axis=0)
    g = (g.astype(F32) * jnp.concatenate(scales, axis=1)).astype(BF16)
    total = lax.dot_general(g, wide, (((1,), (1,)), ((), ())), preferred_element_type=F32)

    @pl.when(i == 0)
    def _():
        acc[...] = total

    @pl.when(i == last)
    def _():
        whole = acc[...] + total
        own_ref[...] = whole[:t] + jnp.dot(r_ref[...], a_ref[...], preferred_element_type=F32)
        other_ref[...] = whole[t:].astype(BF16)


def backward(place, cotangent, other_cotangent, scale, gathered, r, down_t):
    t = cotangent.shape[0]
    n, f, _ = gathered.shape
    whole = lambda i, s: (0, 0)
    step = n // 2
    return pl.pallas_call(
        backward_kernel,
        grid_spec=pltpu.PrefetchScalarGridSpec(
            num_scalar_prefetch=1,
            grid=(2,),
            in_specs=[
                pl.BlockSpec(cotangent.shape, whole),
                pl.BlockSpec((t, step * 128), lambda i, s: (0, i)),
                pl.BlockSpec(scale.shape, whole),
                pl.BlockSpec((step, f, 128), lambda i, s: (i, 0, 0)),
                pl.BlockSpec(r.shape, whole),
                pl.BlockSpec(down_t.shape, whole),
            ],
            out_specs=[pl.BlockSpec((t, f), whole)] * 2,
            scratch_shapes=[pltpu.VMEM((2 * t, f), F32)],
        ),
        out_shape=[
            jax.ShapeDtypeStruct((t, f), F32),
            jax.ShapeDtypeStruct((t, f), BF16),
        ],
        compiler_params=pltpu.CompilerParams(vmem_limit_bytes=40 * 1024 * 1024),
        cost_estimate=pl.CostEstimate(
            flops=4 * t * f * n * 128, bytes_accessed=2 * f * n * 128, transcendentals=0
        ),
        name="backward",
    )(place, cotangent, other_cotangent, scale, gathered, r, down_t)


def swap(x, axis):
    return lax.ppermute(x, axis, [(0, 1), (1, 0)])


def cross(x):
    return lax.ppermute(x, ("w", "v"), [(0, 0), (1, 2), (2, 1), (3, 3)])


def every_other(x, which):
    n = x.shape[-1] // 256
    pick = lambda s: jnp.concatenate(
        [x[..., i * 256 : (i + 1) * 256] for i in range(s, n, 2)], axis=-1
    )
    return jnp.where(which == 0, pick(0), pick(1))


def in_order(which, own, other, axis):
    return jnp.where(
        which == 0,
        jnp.concatenate([own, other], axis=axis),
        jnp.concatenate([other, own], axis=axis),
    )


def fold(x, axis, where):
    n = x.shape[0] // 2
    sent = swap(jnp.where(where == 0, x[n:], x[:n]), axis)
    return jnp.where(where == 0, x[:n], x[n:]) + sent


def scatter(x, axis, where):
    n = lax.axis_size(axis)
    x = x.reshape(n, x.shape[0] // n, x.shape[1])
    block = lambda k: lax.dynamic_index_in_dim(x, (where + k) % n, 0, keepdims=False)
    total = block(0)
    for k in range(1, n):
        total += lax.ppermute(block(k), axis, [(i, (i + k) % n) for i in range(n)])
    return total


def second_kernel(i_ref, w_ref, a_ref, b_ref, x_ref, m_ref, o_ref):
    rank = a_ref.shape[0]
    whole = w_ref[...].astype(F32) + lax.dot_general(
        a_ref[...], b_ref[0], (((0,), (0,)), ((), ())), preferred_element_type=F32
    )
    left = jnp.sum(whole * whole, axis=0, keepdims=True)
    pieces = []
    for _ in range(3):
        pieces.append(left.astype(BF16))
        left = left - pieces[-1].astype(F32)
    r = lax.dot_general(
        a_ref[...], x_ref[...], (((1,), (1,)), ((), ())), preferred_element_type=F32
    )
    block = jnp.concatenate(
        [r.astype(BF16)] + pieces + [m_ref[...], jnp.zeros((3, 128), BF16)], axis=0
    )
    for i in range(o_ref.shape[0]):
        o_ref[i] = block


def second_blocks(index, w, down_t, up, tokens, magnitude):
    (n, rank, _), f = up.shape, down_t.shape[1]
    whole = lambda i, s: (0, 0)
    return pl.pallas_call(
        second_kernel,
        grid_spec=pltpu.PrefetchScalarGridSpec(
            num_scalar_prefetch=1,
            grid=(1,),
            in_specs=[
                pl.BlockSpec(w.shape, whole),
                pl.BlockSpec(down_t.shape, whole),
                pl.BlockSpec((1, rank, 128), lambda i, s: (s[0], 0, 0)),
                pl.BlockSpec(tokens.shape, whole),
                pl.BlockSpec((2, 128), whole),
            ],
            out_specs=pl.BlockSpec((n, rank + 8, 128), lambda i, s: (0, 0, 0)),
        ),
        out_shape=jax.ShapeDtypeStruct((n, rank + 8, 128), BF16),
        name="second_blocks",
    )(index.reshape(1), w, down_t, up, tokens, magnitude.reshape(2, 128))


def on_device(tokens, frozen_matrix, adapter_down_factor, adapter_up_factor, magnitude, cotangent):
    t, f = tokens.shape
    n_dp, n_tp = lax.axis_size(DP), lax.axis_size(TP)
    g, h, w, c, z, u, v = (lax.axis_index(a) for a in DP + TP)
    rank, own = adapter_up_factor.shape
    down_t = adapter_down_factor.T
    place = jnp.stack([w, c])
    tie = lax.optimization_barrier

    gathered = lax.all_gather(frozen_matrix, ("g", "h", "c"), axis=0)

    own_half = jnp.where(c == 0, adapter_up_factor[:, :128], adapter_up_factor[:, 128:])
    own_half = spread(own_half, TP)
    cotangent_out = every_other(cotangent, 1 - w)
    cotangent_out, tokens_out = tie((cotangent_out, tokens))
    other_tokens = swap(tokens_out, "w")

    index = (2 * g + h) * 2 + w
    second = second_blocks(index, frozen_matrix, down_t, own_half, tokens, magnitude)
    second, cotangent_out, own_half = tie((second, cotangent_out, own_half))
    second = lax.all_to_all(second, TP, 0, 0)
    squares = second[:, rank : rank + 3].astype(F32)
    squares = jnp.sum(squares, axis=(0, 1)).reshape(1, 128)
    other_half = swap(own_half, "c")
    up_blocks = in_order(c, own_half[:, None], other_half[:, None], 1)
    full_up = jnp.moveaxis(up_blocks, 2, 0).reshape(rank, -1)

    squares = spread(squares, DP)
    rank_activation = jnp.sum(second[:, :rank].astype(F32), axis=0).astype(BF16)
    full_magnitude = second[:, rank + 3 : rank + 5].reshape(-1)
    other_cotangent = swap(cotangent_out, "w")
    outgoing = forward(place, tokens, other_tokens, down_t, own_half, other_half, gathered)
    squares, outgoing, other_cotangent = tie((squares, outgoing, other_cotangent))

    parts = lax.all_to_all(outgoing, TP, 0, 0)

    norm = jnp.sqrt(squares.reshape(-1) + epsilon)
    scale = full_magnitude.astype(F32) / norm
    scaled = (cotangent.astype(F32) * scale).astype(BF16)
    rank_back = lax.dot_general(
        scaled, full_up, (((1,), (1,)), ((), ())), preferred_element_type=F32
    ).astype(BF16)
    down = lax.dot_general(
        rank_back, tokens, (((0,), (0,)), ((), ())), preferred_element_type=F32
    )
    q = (2 * z + u) * 2 + v
    up = jnp.dot(
        rank_activation,
        lax.dynamic_slice_in_dim(scaled, q * own, own, 1),
        preferred_element_type=F32,
    )
    shares = jnp.concatenate([down, up], axis=1)
    shares = fold(fold(shares, "c", c), "h", h)
    shares = scatter(shares, "g", g)

    shares, rank_back = tie((shares, rank_back))
    own_part, other_part = backward(
        place, cotangent, other_cotangent, scale.reshape(1, -1), gathered, rank_back, down_t
    )
    shares = fold(shares, "w", w)
    parts, other_part = tie((parts, other_part))

    block = 2 * z + u
    here = 2 * block + w
    at = lambda x: lax.dynamic_slice_in_dim(x, here * own, own, 0)
    merged = jnp.sum(parts.astype(F32), axis=0)
    here_cotangent = jnp.where(
        v == w,
        lax.dynamic_slice_in_dim(cotangent, here * own, own, 1),
        lax.dynamic_slice_in_dim(other_cotangent, block * own, own, 1),
    ).astype(F32)
    mag_part = jnp.sum(here_cotangent * merged, axis=0) / at(norm)

    high = lax.reduce_precision(mag_part, 8, 7)
    mag_part = jnp.stack([high, mag_part - high]).astype(BF16)
    last = jnp.concatenate([shares.astype(BF16), mag_part], axis=1)
    last, merged, other_part = tie((last, merged, other_part))
    last = spread(last, ("c", "h", "g", "w", "v")).reshape(n_dp // 2, 2, 2, 2, f + 2 * own)
    factor = 1.0 / math.sqrt(t * n_dp)
    sums = last[..., : f + own]
    sums = jnp.where(v == 0, sums[:, :, 0], sums[:, :, 1]).astype(F32)
    sums = sums.reshape(rank, f + own) * factor
    grad_down = sums[:, :f].T
    grad_up = sums[:, f:]
    mags = last[..., f + own :]
    mags = jnp.where(v == 0, mags[:, 0], mags[:, 1]).astype(F32)
    grad_magnitude = jnp.sum(mags, axis=(0, 1, 2)) * factor

    here_output = (merged * at(scale)).astype(BF16)
    output = jnp.where(v == w, here_output, cross(here_output))
    input_gradient = (own_part + swap(other_part, "w").astype(F32)).astype(BF16)
    return (output, input_gradient, grad_down, grad_up, grad_magnitude)


def solution(mesh):
    fine = Mesh(mesh.devices.reshape(4, 2, 2, 2, 4, 2, 2), DP + TP)
    return jax.shard_map(
        on_device,
        mesh=fine,
        in_specs=(P(DP, TP), P(TP, DP), P(TP, None), P(None, TP), P(TP), P(DP, None)),
        out_specs=(P(DP, TP), P(DP, TP), P(TP, None), P(None, TP), P(TP)),
        check_vma=False,
    )
```

```python
import math

import jax
import jax.numpy as jnp
from jax import lax
from jax.experimental import pallas as pl
from jax.experimental.pallas import tpu as pltpu
from jax.sharding import Mesh
from jax.sharding import PartitionSpec as P

epsilon = 1e-06
F32 = jnp.float32
BF16 = jnp.bfloat16
DP = ("g", "h", "w", "c")
TP = ("z", "u", "v")


def spread(block, axis):
    n = lax.axis_size(axis)
    return lax.all_to_all(jnp.broadcast_to(block[None], (n,) + block.shape), axis, 0, 0)


def forward_kernel(i_ref, x_ref, o_ref, a_ref, b_ref, c_ref, w_ref, *rest):
    w, c = i_ref[0], i_ref[1]
    out, x, r = rest
    t = x_ref.shape[0]

    @pl.when(pl.program_id(0) == 0)
    def _():
        x[:t] = jnp.where(w == 0, x_ref[...], o_ref[...])
        x[t:] = jnp.where(w == 0, o_ref[...], x_ref[...])
        r[...] = lax.dot_general(
            x[...], a_ref[...], (((1,), (1,)), ((), ())), preferred_element_type=F32
        ).astype(BF16)

    for k in range(2):
        b, d = b_ref[2 * k + w], c_ref[2 * k + w]
        up = jnp.concatenate([jnp.where(c == 0, b, d), jnp.where(c == 0, d, b)], axis=1)
        wide = jnp.concatenate([w_ref[2 * k], w_ref[2 * k + 1]], axis=1)
        y = jnp.dot(x[...], wide, preferred_element_type=F32)
        y = (y + jnp.dot(r[...], up, preferred_element_type=F32)).astype(BF16)
        out[2 * k] = y[:t]
        out[2 * k + 1] = y[t:]


def forward(place, x, other_x, down_t, up, other_up, gathered):
    t, f = x.shape
    n, rank = gathered.shape[0], down_t.shape[0]
    whole = lambda i, s: (0, 0)
    part = lambda i, s: (i, 0, 0)
    return pl.pallas_call(
        forward_kernel,
        grid_spec=pltpu.PrefetchScalarGridSpec(
            num_scalar_prefetch=1,
            grid=(n // 4,),
            in_specs=[
                pl.BlockSpec((t, f), whole),
                pl.BlockSpec((t, f), whole),
                pl.BlockSpec((rank, f), whole),
                pl.BlockSpec((4, rank, 128), part),
                pl.BlockSpec((4, rank, 128), part),
                pl.BlockSpec((4, f, 128), part),
            ],
            out_specs=pl.BlockSpec((4, t, 256), part),
            scratch_shapes=[pltpu.VMEM((2 * t, f), BF16), pltpu.VMEM((2 * t, rank), BF16)],
        ),
        out_shape=jax.ShapeDtypeStruct((n, t, 256), BF16),
        cost_estimate=pl.CostEstimate(
            flops=4 * t * f * n * 128, bytes_accessed=2 * f * n * 128, transcendentals=0
        ),
        name="forward",
    )(place, x, other_x, down_t, up, other_up, gathered)


def backward_kernel(i_ref, g_ref, h_ref, s_ref, w_ref, r_ref, a_ref, own_ref, other_ref, acc):
    i, last = pl.program_id(0), pl.num_programs(0) - 1
    t, n = g_ref.shape[0], w_ref.shape[0]
    wide = jnp.concatenate([w_ref[k] for k in range(n)], axis=1)
    rows, scales = [], []
    for k in range(n // 2):
        mine = pl.ds(pl.multiple_of((n * i + 2 * k + i_ref[0]) * 256, 256), 256)
        rows.append(g_ref[:, mine])
        scales.append(s_ref[:, mine])
    g = jnp.concatenate([jnp.concatenate(rows, axis=1), h_ref[...]], axis=0)
    g = (g.astype(F32) * jnp.concatenate(scales, axis=1)).astype(BF16)
    total = lax.dot_general(g, wide, (((1,), (1,)), ((), ())), preferred_element_type=F32)

    @pl.when(i == 0)
    def _():
        acc[...] = total

    @pl.when(i == last)
    def _():
        whole = acc[...] + total
        own_ref[...] = whole[:t] + jnp.dot(r_ref[...], a_ref[...], preferred_element_type=F32)
        other_ref[...] = whole[t:].astype(BF16)


def backward(place, cotangent, other_cotangent, scale, gathered, r, down_t):
    t = cotangent.shape[0]
    n, f, _ = gathered.shape
    whole = lambda i, s: (0, 0)
    step = n // 2
    return pl.pallas_call(
        backward_kernel,
        grid_spec=pltpu.PrefetchScalarGridSpec(
            num_scalar_prefetch=1,
            grid=(2,),
            in_specs=[
                pl.BlockSpec(cotangent.shape, whole),
                pl.BlockSpec((t, step * 128), lambda i, s: (0, i)),
                pl.BlockSpec(scale.shape, whole),
                pl.BlockSpec((step, f, 128), lambda i, s: (i, 0, 0)),
                pl.BlockSpec(r.shape, whole),
                pl.BlockSpec(down_t.shape, whole),
            ],
            out_specs=[pl.BlockSpec((t, f), whole)] * 2,
            scratch_shapes=[pltpu.VMEM((2 * t, f), F32)],
        ),
        out_shape=[
            jax.ShapeDtypeStruct((t, f), F32),
            jax.ShapeDtypeStruct((t, f), BF16),
        ],
        compiler_params=pltpu.CompilerParams(vmem_limit_bytes=40 * 1024 * 1024),
        cost_estimate=pl.CostEstimate(
            flops=4 * t * f * n * 128, bytes_accessed=2 * f * n * 128, transcendentals=0
        ),
        name="backward",
    )(place, cotangent, other_cotangent, scale, gathered, r, down_t)


def swap(x, axis):
    return lax.ppermute(x, axis, [(0, 1), (1, 0)])


def cross(x):
    return lax.ppermute(x, ("w", "v"), [(0, 0), (1, 2), (2, 1), (3, 3)])


def every_other(x, which):
    n = x.shape[-1] // 256
    pick = lambda s: jnp.concatenate(
        [x[..., i * 256 : (i + 1) * 256] for i in range(s, n, 2)], axis=-1
    )
    return jnp.where(which == 0, pick(0), pick(1))


def in_order(which, own, other, axis):
    return jnp.where(
        which == 0,
        jnp.concatenate([own, other], axis=axis),
        jnp.concatenate([other, own], axis=axis),
    )


def fold(x, axis, where):
    n = x.shape[0] // 2
    sent = swap(jnp.where(where == 0, x[n:], x[:n]), axis)
    return jnp.where(where == 0, x[:n], x[n:]) + sent


def scatter(x, axis, where):
    n = lax.axis_size(axis)
    x = x.reshape(n, x.shape[0] // n, x.shape[1])
    block = lambda k: lax.dynamic_index_in_dim(x, (where + k) % n, 0, keepdims=False)
    total = block(0)
    for k in range(1, n):
        total += lax.ppermute(block(k), axis, [(i, (i + k) % n) for i in range(n)])
    return total


def second_kernel(i_ref, w_ref, a_ref, b_ref, x_ref, m_ref, o_ref):
    rank = a_ref.shape[0]
    whole = w_ref[...].astype(F32) + lax.dot_general(
        a_ref[...], b_ref[0], (((0,), (0,)), ((), ())), preferred_element_type=F32
    )
    left = jnp.sum(whole * whole, axis=0, keepdims=True)
    pieces = []
    for _ in range(3):
        pieces.append(left.astype(BF16))
        left = left - pieces[-1].astype(F32)
    r = lax.dot_general(
        a_ref[...], x_ref[...], (((1,), (1,)), ((), ())), preferred_element_type=F32
    )
    block = jnp.concatenate(
        [r.astype(BF16)] + pieces + [m_ref[...], jnp.zeros((3, 128), BF16)], axis=0
    )
    for i in range(o_ref.shape[0]):
        o_ref[i] = block


def second_blocks(index, w, down_t, up, tokens, magnitude):
    (n, rank, _), f = up.shape, down_t.shape[1]
    whole = lambda i, s: (0, 0)
    return pl.pallas_call(
        second_kernel,
        grid_spec=pltpu.PrefetchScalarGridSpec(
            num_scalar_prefetch=1,
            grid=(1,),
            in_specs=[
                pl.BlockSpec(w.shape, whole),
                pl.BlockSpec(down_t.shape, whole),
                pl.BlockSpec((1, rank, 128), lambda i, s: (s[0], 0, 0)),
                pl.BlockSpec(tokens.shape, whole),
                pl.BlockSpec((2, 128), whole),
            ],
            out_specs=pl.BlockSpec((n, rank + 8, 128), lambda i, s: (0, 0, 0)),
        ),
        out_shape=jax.ShapeDtypeStruct((n, rank + 8, 128), BF16),
        name="second_blocks",
    )(index.reshape(1), w, down_t, up, tokens, magnitude.reshape(2, 128))


def on_device(tokens, frozen_matrix, adapter_down_factor, adapter_up_factor, magnitude, cotangent):
    t, f = tokens.shape
    n_dp, n_tp = lax.axis_size(DP), lax.axis_size(TP)
    g, h, w, c, z, u, v = (lax.axis_index(a) for a in DP + TP)
    rank, own = adapter_up_factor.shape
    down_t = adapter_down_factor.T
    place = jnp.stack([w, c])
    tie = lax.optimization_barrier

    gathered = lax.all_gather(frozen_matrix, ("g", "h", "c"), axis=0)

    own_half = jnp.where(c == 0, adapter_up_factor[:, :128], adapter_up_factor[:, 128:])
    own_half = spread(own_half, TP)
    cotangent_out = every_other(cotangent, 1 - w)
    cotangent_out, tokens_out = tie((cotangent_out, tokens))
    other_tokens = swap(tokens_out, "w")

    index = (2 * g + h) * 2 + w
    second = second_blocks(index, frozen_matrix, down_t, own_half, tokens, magnitude)
    second, cotangent_out = tie((second, cotangent_out))
    second = lax.all_to_all(second, TP, 0, 0)
    squares = second[:, rank : rank + 3].astype(F32)
    squares = jnp.sum(squares, axis=(0, 1)).reshape(1, 128)
    other_half = swap(own_half, "c")
    up_blocks = in_order(c, own_half[:, None], other_half[:, None], 1)
    full_up = jnp.moveaxis(up_blocks, 2, 0).reshape(rank, -1)

    squares = spread(squares, DP)
    rank_activation = jnp.sum(second[:, :rank].astype(F32), axis=0).astype(BF16)
    full_magnitude = second[:, rank + 3 : rank + 5].reshape(-1)
    other_cotangent = swap(cotangent_out, "w")
    outgoing = forward(place, tokens, other_tokens, down_t, own_half, other_half, gathered)
    squares, outgoing, other_cotangent = tie((squares, outgoing, other_cotangent))

    parts = lax.all_to_all(outgoing, TP, 0, 0)

    norm = jnp.sqrt(squares.reshape(-1) + epsilon)
    scale = full_magnitude.astype(F32) / norm
    scaled = (cotangent.astype(F32) * scale).astype(BF16)
    rank_back = lax.dot_general(
        scaled, full_up, (((1,), (1,)), ((), ())), preferred_element_type=F32
    ).astype(BF16)
    down = lax.dot_general(
        rank_back, tokens, (((0,), (0,)), ((), ())), preferred_element_type=F32
    )
    q = (2 * z + u) * 2 + v
    up = jnp.dot(
        rank_activation,
        lax.dynamic_slice_in_dim(scaled, q * own, own, 1),
        preferred_element_type=F32,
    )
    shares = jnp.concatenate([down, up], axis=1)
    shares = fold(fold(shares, "c", c), "h", h)
    shares = scatter(shares, "g", g)

    shares, rank_back = tie((shares, rank_back))
    own_part, other_part = backward(
        place, cotangent, other_cotangent, scale.reshape(1, -1), gathered, rank_back, down_t
    )
    shares = fold(shares, "w", w)
    parts, other_part = tie((parts, other_part))

    block = 2 * z + u
    here = 2 * block + w
    at = lambda x: lax.dynamic_slice_in_dim(x, here * own, own, 0)
    merged = jnp.sum(parts.astype(F32), axis=0)
    here_cotangent = jnp.where(
        v == w,
        lax.dynamic_slice_in_dim(cotangent, here * own, own, 1),
        lax.dynamic_slice_in_dim(other_cotangent, block * own, own, 1),
    ).astype(F32)
    factor = 1.0 / math.sqrt(t * n_dp)
    mag_part = jnp.sum(here_cotangent * merged, axis=0) / at(norm) * factor

    high = lax.reduce_precision(mag_part, 8, 7)
    mag_part = jnp.stack([high, mag_part - high]).astype(BF16)
    last = jnp.concatenate([shares.astype(BF16), mag_part], axis=1)
    last, merged, other_part = tie((last, merged, other_part))
    last = spread(last, ("c", "h", "g", "w", "v")).reshape(n_dp // 2, 2, 2, 2, f + 2 * own)
    sums = last[..., : f + own]
    sums = jnp.where(v == 0, sums[:, :, 0], sums[:, :, 1]).astype(F32)
    sums = sums.reshape(rank, f + own) * factor
    grad_down = sums[:, :f].T
    grad_up = sums[:, f:]
    mags = last[..., f + own :]
    mags = jnp.where(v == 0, mags[:, 0], mags[:, 1]).astype(F32)
    grad_magnitude = jnp.sum(mags, axis=(0, 1, 2))

    here_output = (merged * at(scale)).astype(BF16)
    output = jnp.where(v == w, here_output, cross(here_output))
    input_gradient = (own_part + swap(other_part, "w").astype(F32)).astype(BF16)
    return (output, input_gradient, grad_down, grad_up, grad_magnitude)


def solution(mesh):
    fine = Mesh(mesh.devices.reshape(4, 2, 2, 2, 4, 2, 2), DP + TP)
    return jax.shard_map(
        on_device,
        mesh=fine,
        in_specs=(P(DP, TP), P(TP, DP), P(TP, None), P(None, TP), P(TP), P(DP, None)),
        out_specs=(P(DP, TP), P(DP, TP), P(TP, None), P(None, TP), P(TP)),
        check_vma=False,
    )
```

```python
import math

import jax
import jax.numpy as jnp
from jax import lax
from jax.experimental import pallas as pl
from jax.experimental.pallas import tpu as pltpu
from jax.sharding import Mesh
from jax.sharding import PartitionSpec as P

epsilon = 1e-06
F32 = jnp.float32
BF16 = jnp.bfloat16
DP = ("g", "h", "w", "c")
TP = ("z", "u", "v")


def spread(block, axis):
    n = lax.axis_size(axis)
    return lax.all_to_all(jnp.broadcast_to(block[None], (n,) + block.shape), axis, 0, 0)


def forward_kernel(i_ref, x_ref, o_ref, a_ref, b_ref, c_ref, w_ref, *rest):
    w, c = i_ref[0], i_ref[1]
    out, x, r = rest
    t = x_ref.shape[0]

    @pl.when(pl.program_id(0) == 0)
    def _():
        x[:t] = jnp.where(w == 0, x_ref[...], o_ref[...])
        x[t:] = jnp.where(w == 0, o_ref[...], x_ref[...])
        r[...] = lax.dot_general(
            x[...], a_ref[...], (((1,), (1,)), ((), ())), preferred_element_type=F32
        ).astype(BF16)

    n = w_ref.shape[0]
    ups = []
    for k in range(n // 2):
        b, d = b_ref[2 * k + w], c_ref[2 * k + w]
        ups += [jnp.where(c == 0, b, d), jnp.where(c == 0, d, b)]
    wide = jnp.concatenate([w_ref[k] for k in range(n)], axis=1)
    y = jnp.dot(x[...], wide, preferred_element_type=F32)
    y = y + jnp.dot(r[...], jnp.concatenate(ups, axis=1), preferred_element_type=F32)
    y = y.astype(BF16)
    for k in range(n // 2):
        out[2 * k] = y[:t, k * 256 : (k + 1) * 256]
        out[2 * k + 1] = y[t:, k * 256 : (k + 1) * 256]


def forward(place, x, other_x, down_t, up, other_up, gathered):
    t, f = x.shape
    n, rank = gathered.shape[0], down_t.shape[0]
    whole = lambda i, s: (0, 0)
    part = lambda i, s: (i, 0, 0)
    return pl.pallas_call(
        forward_kernel,
        grid_spec=pltpu.PrefetchScalarGridSpec(
            num_scalar_prefetch=1,
            grid=(n // 8,),
            in_specs=[
                pl.BlockSpec((t, f), whole),
                pl.BlockSpec((t, f), whole),
                pl.BlockSpec((rank, f), whole),
                pl.BlockSpec((8, rank, 128), part),
                pl.BlockSpec((8, rank, 128), part),
                pl.BlockSpec((8, f, 128), part),
            ],
            out_specs=pl.BlockSpec((8, t, 256), part),
            scratch_shapes=[pltpu.VMEM((2 * t, f), BF16), pltpu.VMEM((2 * t, rank), BF16)],
        ),
        out_shape=jax.ShapeDtypeStruct((n, t, 256), BF16),
        compiler_params=pltpu.CompilerParams(vmem_limit_bytes=40 * 1024 * 1024),
        cost_estimate=pl.CostEstimate(
            flops=4 * t * f * n * 128, bytes_accessed=2 * f * n * 128, transcendentals=0
        ),
        name="forward",
    )(place, x, other_x, down_t, up, other_up, gathered)


def backward_kernel(i_ref, g_ref, h_ref, s_ref, w_ref, r_ref, a_ref, own_ref, other_ref, acc):
    i, last = pl.program_id(0), pl.num_programs(0) - 1
    t, n = g_ref.shape[0], w_ref.shape[0]
    wide = jnp.concatenate([w_ref[k] for k in range(n)], axis=1)
    rows, scales = [], []
    for k in range(n // 2):
        mine = pl.ds(pl.multiple_of((n * i + 2 * k + i_ref[0]) * 256, 256), 256)
        rows.append(g_ref[:, mine])
        scales.append(s_ref[:, mine])
    g = jnp.concatenate([jnp.concatenate(rows, axis=1), h_ref[...]], axis=0)
    g = (g.astype(F32) * jnp.concatenate(scales, axis=1)).astype(BF16)
    total = lax.dot_general(g, wide, (((1,), (1,)), ((), ())), preferred_element_type=F32)

    @pl.when(i == 0)
    def _():
        acc[...] = total

    @pl.when(i == last)
    def _():
        whole = acc[...] + total
        own_ref[...] = whole[:t] + jnp.dot(r_ref[...], a_ref[...], preferred_element_type=F32)
        other_ref[...] = whole[t:].astype(BF16)


def backward(place, cotangent, other_cotangent, scale, gathered, r, down_t):
    t = cotangent.shape[0]
    n, f, _ = gathered.shape
    whole = lambda i, s: (0, 0)
    step = n // 2
    return pl.pallas_call(
        backward_kernel,
        grid_spec=pltpu.PrefetchScalarGridSpec(
            num_scalar_prefetch=1,
            grid=(2,),
            in_specs=[
                pl.BlockSpec(cotangent.shape, whole),
                pl.BlockSpec((t, step * 128), lambda i, s: (0, i)),
                pl.BlockSpec(scale.shape, whole),
                pl.BlockSpec((step, f, 128), lambda i, s: (i, 0, 0)),
                pl.BlockSpec(r.shape, whole),
                pl.BlockSpec(down_t.shape, whole),
            ],
            out_specs=[pl.BlockSpec((t, f), whole)] * 2,
            scratch_shapes=[pltpu.VMEM((2 * t, f), F32)],
        ),
        out_shape=[
            jax.ShapeDtypeStruct((t, f), F32),
            jax.ShapeDtypeStruct((t, f), BF16),
        ],
        compiler_params=pltpu.CompilerParams(vmem_limit_bytes=40 * 1024 * 1024),
        cost_estimate=pl.CostEstimate(
            flops=4 * t * f * n * 128, bytes_accessed=2 * f * n * 128, transcendentals=0
        ),
        name="backward",
    )(place, cotangent, other_cotangent, scale, gathered, r, down_t)


def swap(x, axis):
    return lax.ppermute(x, axis, [(0, 1), (1, 0)])


def cross(x):
    return lax.ppermute(x, ("w", "v"), [(0, 0), (1, 2), (2, 1), (3, 3)])


def every_other(x, which):
    n = x.shape[-1] // 256
    pick = lambda s: jnp.concatenate(
        [x[..., i * 256 : (i + 1) * 256] for i in range(s, n, 2)], axis=-1
    )
    return jnp.where(which == 0, pick(0), pick(1))


def in_order(which, own, other, axis):
    return jnp.where(
        which == 0,
        jnp.concatenate([own, other], axis=axis),
        jnp.concatenate([other, own], axis=axis),
    )


def fold(x, axis, where):
    n = x.shape[0] // 2
    sent = swap(jnp.where(where == 0, x[n:], x[:n]), axis)
    return jnp.where(where == 0, x[:n], x[n:]) + sent


def scatter(x, axis, where):
    n = lax.axis_size(axis)
    x = x.reshape(n, x.shape[0] // n, x.shape[1])
    block = lambda k: lax.dynamic_index_in_dim(x, (where + k) % n, 0, keepdims=False)
    total = block(0)
    for k in range(1, n):
        total += lax.ppermute(block(k), axis, [(i, (i + k) % n) for i in range(n)])
    return total


def second_kernel(i_ref, w_ref, a_ref, b_ref, x_ref, m_ref, o_ref):
    rank = a_ref.shape[0]
    whole = w_ref[...].astype(F32) + lax.dot_general(
        a_ref[...], b_ref[0], (((0,), (0,)), ((), ())), preferred_element_type=F32
    )
    left = jnp.sum(whole * whole, axis=0, keepdims=True)
    pieces = []
    for _ in range(3):
        pieces.append(left.astype(BF16))
        left = left - pieces[-1].astype(F32)
    r = lax.dot_general(
        a_ref[...], x_ref[...], (((1,), (1,)), ((), ())), preferred_element_type=F32
    )
    block = jnp.concatenate(
        [r.astype(BF16)] + pieces + [m_ref[...], jnp.zeros((3, 128), BF16)], axis=0
    )
    for i in range(o_ref.shape[0]):
        o_ref[i] = block


def second_blocks(index, w, down_t, up, tokens, magnitude):
    (n, rank, _), f = up.shape, down_t.shape[1]
    whole = lambda i, s: (0, 0)
    return pl.pallas_call(
        second_kernel,
        grid_spec=pltpu.PrefetchScalarGridSpec(
            num_scalar_prefetch=1,
            grid=(1,),
            in_specs=[
                pl.BlockSpec(w.shape, whole),
                pl.BlockSpec(down_t.shape, whole),
                pl.BlockSpec((1, rank, 128), lambda i, s: (s[0], 0, 0)),
                pl.BlockSpec(tokens.shape, whole),
                pl.BlockSpec((2, 128), whole),
            ],
            out_specs=pl.BlockSpec((n, rank + 8, 128), lambda i, s: (0, 0, 0)),
        ),
        out_shape=jax.ShapeDtypeStruct((n, rank + 8, 128), BF16),
        name="second_blocks",
    )(index.reshape(1), w, down_t, up, tokens, magnitude.reshape(2, 128))


def on_device(tokens, frozen_matrix, adapter_down_factor, adapter_up_factor, magnitude, cotangent):
    t, f = tokens.shape
    n_dp, n_tp = lax.axis_size(DP), lax.axis_size(TP)
    g, h, w, c, z, u, v = (lax.axis_index(a) for a in DP + TP)
    rank, own = adapter_up_factor.shape
    down_t = adapter_down_factor.T
    place = jnp.stack([w, c])
    tie = lax.optimization_barrier

    gathered = lax.all_gather(frozen_matrix, ("g", "h", "c"), axis=0)

    own_half = jnp.where(c == 0, adapter_up_factor[:, :128], adapter_up_factor[:, 128:])
    own_half = spread(own_half, TP)
    cotangent_out = every_other(cotangent, 1 - w)
    cotangent_out, tokens_out = tie((cotangent_out, tokens))
    other_tokens = swap(tokens_out, "w")

    index = (2 * g + h) * 2 + w
    second = second_blocks(index, frozen_matrix, down_t, own_half, tokens, magnitude)
    second, cotangent_out = tie((second, cotangent_out))
    second = lax.all_to_all(second, TP, 0, 0)
    squares = second[:, rank : rank + 3].astype(F32)
    squares = jnp.sum(squares, axis=(0, 1)).reshape(1, 128)
    other_half = swap(own_half, "c")
    up_blocks = in_order(c, own_half[:, None], other_half[:, None], 1)
    full_up = jnp.moveaxis(up_blocks, 2, 0).reshape(rank, -1)

    squares = spread(squares, DP)
    rank_activation = jnp.sum(second[:, :rank].astype(F32), axis=0).astype(BF16)
    full_magnitude = second[:, rank + 3 : rank + 5].reshape(-1)
    other_cotangent = swap(cotangent_out, "w")
    outgoing = forward(place, tokens, other_tokens, down_t, own_half, other_half, gathered)
    squares, outgoing, other_cotangent = tie((squares, outgoing, other_cotangent))

    parts = lax.all_to_all(outgoing, TP, 0, 0)

    norm = jnp.sqrt(squares.reshape(-1) + epsilon)
    scale = full_magnitude.astype(F32) / norm
    scaled = (cotangent.astype(F32) * scale).astype(BF16)
    rank_back = lax.dot_general(
        scaled, full_up, (((1,), (1,)), ((), ())), preferred_element_type=F32
    ).astype(BF16)
    down = lax.dot_general(
        rank_back, tokens, (((0,), (0,)), ((), ())), preferred_element_type=F32
    )
    q = (2 * z + u) * 2 + v
    up = jnp.dot(
        rank_activation,
        lax.dynamic_slice_in_dim(scaled, q * own, own, 1),
        preferred_element_type=F32,
    )
    shares = jnp.concatenate([down, up], axis=1)
    shares = fold(fold(shares, "c", c), "h", h)
    shares = scatter(shares, "g", g)

    shares, rank_back = tie((shares, rank_back))
    own_part, other_part = backward(
        place, cotangent, other_cotangent, scale.reshape(1, -1), gathered, rank_back, down_t
    )
    shares = fold(shares, "w", w)
    parts, other_part = tie((parts, other_part))

    block = 2 * z + u
    here = 2 * block + w
    at = lambda x: lax.dynamic_slice_in_dim(x, here * own, own, 0)
    merged = jnp.sum(parts.astype(F32), axis=0)
    here_cotangent = jnp.where(
        v == w,
        lax.dynamic_slice_in_dim(cotangent, here * own, own, 1),
        lax.dynamic_slice_in_dim(other_cotangent, block * own, own, 1),
    ).astype(F32)
    factor = 1.0 / math.sqrt(t * n_dp)
    mag_part = jnp.sum(here_cotangent * merged, axis=0) / at(norm) * factor

    high = lax.reduce_precision(mag_part, 8, 7)
    mag_part = jnp.stack([high, mag_part - high]).astype(BF16)
    last = jnp.concatenate([shares.astype(BF16), mag_part], axis=1)
    last, merged, other_part = tie((last, merged, other_part))
    last = spread(last, ("c", "h", "g", "w", "v")).reshape(n_dp // 2, 2, 2, 2, f + 2 * own)
    sums = last[..., : f + own]
    sums = jnp.where(v == 0, sums[:, :, 0], sums[:, :, 1]).astype(F32)
    sums = sums.reshape(rank, f + own) * factor
    grad_down = sums[:, :f].T
    grad_up = sums[:, f:]
    mags = last[..., f + own :]
    mags = jnp.where(v == 0, mags[:, 0], mags[:, 1]).astype(F32)
    grad_magnitude = jnp.sum(mags, axis=(0, 1, 2))

    here_output = (merged * at(scale)).astype(BF16)
    output = jnp.where(v == w, here_output, cross(here_output))
    input_gradient = (own_part + swap(other_part, "w").astype(F32)).astype(BF16)
    return (output, input_gradient, grad_down, grad_up, grad_magnitude)


def solution(mesh):
    fine = Mesh(mesh.devices.reshape(4, 2, 2, 2, 4, 2, 2), DP + TP)
    return jax.shard_map(
        on_device,
        mesh=fine,
        in_specs=(P(DP, TP), P(TP, DP), P(TP, None), P(None, TP), P(TP), P(DP, None)),
        out_specs=(P(DP, TP), P(DP, TP), P(TP, None), P(None, TP), P(TP)),
        check_vma=False,
    )
```
